32 devices in a mesh: case: 2 (over x), span: 8 (over z, y), dom: 2 (over core).
Axes of the slice: x: 2, y: 2, z: 4, core: 2. Of those that a mesh axis runs over, the one named last changes fastest.
Arguments:
- scalar: float32 [256, 8192], P(('case', 'span'), 'dom'), parts along dimension 0, may hold values from -6 to 6
- span_vel: float32 [256, 8192], P(('case', 'span'), 'dom'), parts along dimension 0, may hold values from -4 to 4
- flux_weight: float32 [4, 8192], P(None, 'dom'), may hold values from -4 to 4
- neighbours: int32 [4, 8192], P(None, 'dom'), may hold values from 0 to 8191, as said below
- diagonal: float32 [8192], P('dom'), may hold values from 0.5 to 2
- interface: int32 [16, 128], P('dom'), may hold values from 0 to 8191, as said below
- schur_one: float32 [128, 8, 128, 128], P('span', 'dom'), may hold values from -1 to 1
- schur_two: float32 [128, 4, 128, 128], P('span', 'dom'), may hold values from -1 to 1
- schur_three: float32 [128, 2, 128, 128], P('span', 'dom'), may hold values from -1 to 1
- schur_root: float32 [128, 1, 128, 128], P('span'), may hold values from -1 to 1
Outputs:
- pressure: float32 [256, 8192], P(('case', 'span'), 'dom'), parts along dimension 0
- corrected: float32 [256, 8192], P(('case', 'span'), 'dom'), parts along dimension 0
The draws below stay inside these ranges and needn't reach their ends.
There are 2 independent parts, one for each index of `case`. The reference program is written for one: setup_inputs(seed, part) draws one part's arguments, and reference() takes and returns one part's arrays. A program takes and returns all parts, laid end to end along the dimension named above; an argument that names none is the same for every part. Nothing has to cross between parts.
Inputs may be any that keep to these rules, and one draw needn't show every extreme that they name: `neighbours`: every entry lies 1 to 64 cells from its own cell in the numbering, and the distance 64 occurs. `interface`: row d holds 128 distinct cells of subdomain d, numbered from d * 512 to (d + 1) * 512 - 1.
All inputs are finite; a program needn't handle non-finite values.
Results may differ from the reference program's by a relative error of at most 0.0001.
Values sent between devices are 32-bit elements; how exact they have to be, the bound alone decides.
A program may use at most 64 MiB of HBM per device.

```python
import math
import jax
import jax.numpy as jnp
from jax import lax

PLANES = 128
DOMAINS = 16
CELL_DOM = 512
B = 128
HALO = 64
NBR = 4
CELLS = 8192


def schur_draw(key, nodes):
    first = jax.random.fold_in(key, 0)
    shape = (PLANES, nodes, B, B)
    identity = jnp.eye(B, dtype=jnp.float32)
    noise = jax.random.normal(first, shape, jnp.float32) * (0.3 / math.sqrt(B))
    return jnp.clip(0.6 * identity + noise, -1.0, 1.0)


def draw_schur_one(key, part):
    return schur_draw(jax.random.fold_in(key, 11), DOMAINS // 2)


def draw_schur_two(key, part):
    return schur_draw(jax.random.fold_in(key, 12), DOMAINS // 4)


def draw_schur_three(key, part):
    return schur_draw(jax.random.fold_in(key, 13), DOMAINS // 8)


def draw_schur_root(key, part):
    return schur_draw(jax.random.fold_in(key, 14), 1)


def draw_neighbours(key, part):
    first, second = jax.random.split(jax.random.fold_in(key, 21))
    cell_ids = jnp.arange(CELLS, dtype=jnp.int32)[None, :]
    lengths = jax.random.randint(first, (NBR, CELLS), 1, HALO + 1)
    lengths = jnp.where(cell_ids % 16 == 0, HALO, lengths)
    signs = jax.random.randint(second, (NBR, CELLS), 0, 2) * 2 - 1
    target = cell_ids + signs * lengths
    outside = (target < 0) | (target >= CELLS)
    target = jnp.where(outside, cell_ids - signs * lengths, target)
    return target.astype(jnp.int32)


def draw_interface(key, part):
    domain_keys = jax.random.split(jax.random.fold_in(key, 31), DOMAINS)
    chosen = jax.vmap(lambda single: jax.random.permutation(single, CELL_DOM)[:B])(domain_keys)
    offsets = jnp.arange(DOMAINS, dtype=jnp.int32)[:, None] * CELL_DOM
    return (chosen + offsets).astype(jnp.int32)


def steps_of(own_key, dims, shards, least, high):
    def one(dim, parts):
        draws = jax.random.uniform(jax.random.fold_in(jax.random.fold_in(own_key, 6), dim), (parts,), jnp.float32, least / len(shards), high / len(shards))
        return jnp.repeat(jnp.exp(draws), dims[dim] // parts).reshape((-1,) + (1,) * (len(dims) - dim - 1))

    loudness = one(*shards[0])
    for cut in shards[1:]:
        loudness = loudness * one(*cut)
    return loudness


def scatter_about(own_key, dims, spread, bound, cuts=(), kind=jnp.bfloat16):
    result = jax.random.normal(own_key, dims, jnp.float32) * spread
    if len(cuts) > 0:
        result = steps_of(own_key, dims, cuts, -0.22, 0.18) * result
    return jnp.clip(result, min=-bound, max=bound).astype(kind)


def setup_inputs(seed: int = 0, part: int = 0) -> dict:
    arg_keys = jax.random.split(jax.random.key(seed), 11)
    part_keys = jax.random.split(jax.random.fold_in(arg_keys[10], part), 11)
    scalar = scatter_about(part_keys[0], (PLANES, CELLS), 1.0, 6.0, ((0, 8), (1, 2)), jnp.float32)
    span_vel = scatter_about(part_keys[1], (PLANES, CELLS), 0.5, 4.0, ((0, 8), (1, 2)), jnp.float32)
    flux_weight = scatter_about(arg_keys[2], (NBR, CELLS), 0.5, 4.0, ((1, 2),), jnp.float32)
    neighbours = draw_neighbours(jax.random.fold_in(arg_keys[10], 71), part)
    diagonal = jnp.clip(0.5 + 1.5 * jax.random.uniform(arg_keys[4], (CELLS,), jnp.float32) ** steps_of(arg_keys[4], (CELLS,), ((0, 2),), -0.2, 0.2), 0.5, 2.0)
    interface = draw_interface(jax.random.fold_in(arg_keys[10], 71), part)
    schur_one = draw_schur_one(jax.random.fold_in(arg_keys[10], 71), part)
    schur_two = draw_schur_two(jax.random.fold_in(arg_keys[10], 71), part)
    schur_three = draw_schur_three(jax.random.fold_in(arg_keys[10], 71), part)
    schur_root = draw_schur_root(jax.random.fold_in(arg_keys[10], 71), part)
    return dict(scalar=scalar, span_vel=span_vel, flux_weight=flux_weight, neighbours=neighbours, diagonal=diagonal, interface=interface, schur_one=schur_one, schur_two=schur_two, schur_three=schur_three, schur_root=schur_root)


def fourier_entry(wave_ids, plane_ids):
    middle = PLANES // 2
    wave_num = jnp.where(wave_ids <= middle, wave_ids, wave_ids - middle)
    phase_angle = (wave_num * plane_ids % PLANES).astype(jnp.float32) * (2.0 * math.pi / PLANES)
    at_edge = (wave_ids == 0) | (wave_ids == middle)
    weight_row = jnp.where(at_edge, math.sqrt(1.0 / PLANES), math.sqrt(2.0 / PLANES))
    return jnp.where(wave_ids <= middle, jnp.cos(phase_angle), jnp.sin(phase_angle)) * weight_row

def wave_shift(wave_ids):
    middle = PLANES // 2
    wave_num = jnp.where(wave_ids <= middle, wave_ids, wave_ids - middle).astype(jnp.float32)
    return (2.0 * jnp.sin(wave_num * (math.pi / PLANES))) ** 2

def stencil(field, span_vel, flux_weight, neighbours):
    ahead = jnp.roll(field, -1, 0)
    behind = jnp.roll(field, 1, 0)
    convected = span_vel * 0.5 * (ahead - behind)
    for slot in range(NBR):
        convected = convected + flux_weight[slot] * (field[:, neighbours[slot]] - field)
    return convected

def reference(scalar, span_vel, flux_weight, neighbours, diagonal, interface, schur_one, schur_two, schur_three, schur_root):
    source = scalar - stencil(scalar, span_vel, flux_weight, neighbours)
    wave_ids = jnp.arange(PLANES, dtype=jnp.int32)
    wave_table = fourier_entry(wave_ids[:, None], wave_ids[None, :])
    spectrum = jnp.dot(wave_table, source, precision=lax.Precision.HIGHEST)
    interior = spectrum / (diagonal[None, :] + wave_shift(wave_ids)[:, None])
    leaves = interior[:, interface]
    levels = [leaves]
    current = leaves
    for blocks in (schur_one, schur_two, schur_three):
        paired = current[:, 0::2] + current[:, 1::2]
        current = jnp.einsum('mnij,mnj->mni', blocks, paired, precision=lax.Precision.HIGHEST)
        levels.append(current)
    paired = current[:, 0::2] + current[:, 1::2]
    top_value = jnp.einsum('mnij,mnj->mni', schur_root, paired, precision=lax.Precision.HIGHEST)
    returned = jnp.einsum('mnji,mnj->mni', schur_root, top_value, precision=lax.Precision.HIGHEST)
    lowered = levels[3] - jnp.repeat(returned, 2, axis=1)
    for blocks, below in ((schur_three, levels[2]), (schur_two, levels[1]), (schur_one, levels[0])):
        returned = jnp.einsum('mnji,mnj->mni', blocks, lowered, precision=lax.Precision.HIGHEST)
        lowered = below - jnp.repeat(returned, 2, axis=1)
    corrected_spectrum = interior.at[:, interface].add(-0.5 * lowered)
    pressure = jnp.dot(wave_table.T, corrected_spectrum, precision=lax.Precision.HIGHEST)
    corrected = scalar - stencil(pressure, span_vel, flux_weight, neighbours)
    return (pressure, corrected)
```

```python
import math

import jax
import jax.numpy as jnp
from jax import lax
from jax.sharding import PartitionSpec as P

PLANES = 128
CELL_DOM = 512
HALO = 64


def extended(value, sides, width, wrap):
    for axis, dim in sides:
        count, length = (lax.axis_size(axis), value.shape[dim])
        up = [(i, (i + 1) % count) for i in range(count if wrap else count - 1)]
        down = [(j, i) for i, j in up]
        last = lax.slice_in_dim(value, length - width, length, axis=dim)
        initial = lax.slice_in_dim(value, 0, width, axis=dim)
        before = lax.ppermute(last, axis, up)
        after = lax.ppermute(initial, axis, down)
        value = jnp.concatenate([before, value, after], axis=dim)
    return value


def swapped(value, axis, distance):
    return lax.ppermute(value, axis, [(i, i ^ 1 << distance) for i in range(lax.axis_size(axis))])


def fourier_entry(wave_ids, plane_ids):
    middle = PLANES // 2
    wave_num = jnp.where(wave_ids <= middle, wave_ids, wave_ids - middle)
    phase_angle = (wave_num * plane_ids % PLANES).astype(jnp.float32) * (2.0 * math.pi / PLANES)
    at_edge = (wave_ids == 0) | (wave_ids == middle)
    weight_row = jnp.where(at_edge, math.sqrt(1.0 / PLANES), math.sqrt(2.0 / PLANES))
    return jnp.where(wave_ids <= middle, jnp.cos(phase_angle), jnp.sin(phase_angle)) * weight_row


def wave_shift(wave_ids):
    middle = PLANES // 2
    wave_num = jnp.where(wave_ids <= middle, wave_ids, wave_ids - middle).astype(jnp.float32)
    return (2.0 * jnp.sin(wave_num * (math.pi / PLANES))) ** 2


def stencil(field, span_vel, flux_weight, near_local):
    planes_ext = extended(field, (("span", 0),), 1, True)
    convected = span_vel * 0.5 * (planes_ext[2:] - planes_ext[:-2])
    widened = extended(field, (("dom", 1),), HALO, False)
    for slot in range(flux_weight.shape[0]):
        convected = convected + flux_weight[slot] * (widened[:, near_local[slot]] - field)
    return convected


def apply_table(table, block):
    return jnp.einsum("rp,pxc->rxc", table, block, precision=lax.Precision.HIGHEST)


def on_device(
    scalar,
    span_vel,
    flux_weight,
    neighbours,
    diagonal,
    interface,
    schur_one,
    schur_two,
    schur_three,
    schur_root,
):
    plane_count = scalar.shape[0]
    cell_count = scalar.shape[1]
    span_count = lax.axis_size("span")
    span_pos = lax.axis_index("span")
    cols_count = cell_count // span_count
    cell_start = lax.axis_index("dom") * cell_count
    near_local = neighbours - cell_start + HALO
    source = scalar - stencil(scalar, span_vel, flux_weight, near_local)
    all_waves = jnp.arange(PLANES, dtype=jnp.int32)
    local_iface = interface - cell_start
    wave_table = fourier_entry(all_waves[:, None], all_waves[None, :])
    slot_count = min(cols_count, interface.shape[1] * max(1, cols_count // CELL_DOM))
    grouped = source.reshape(plane_count, span_count, cols_count)
    spectrum_cols = apply_table(
        wave_table, lax.all_to_all(grouped, "span", split_axis=1, concat_axis=0, tiled=True)
    ).reshape(PLANES, cols_count)
    diag_cols = lax.dynamic_slice_in_dim(diagonal, span_pos * cols_count, cols_count)
    interior_cols = spectrum_cols / (diag_cols[None, :] + wave_shift(all_waves)[:, None])
    flat_iface = local_iface.reshape(-1)
    owner = flat_iface // cols_count
    order = jnp.arange(flat_iface.shape[0], dtype=jnp.int32)
    earlier = (owner[:, None] == owner[None, :]) & (order[None, :] < order[:, None])
    ranks = jnp.sum(earlier.astype(jnp.int32), 1)
    slot_index = owner * slot_count + ranks
    owned = owner == span_pos
    slot_cell = (
        jnp.full((slot_count,), cols_count, jnp.int32)
        .at[jnp.where(owned, ranks, slot_count)]
        .set(flat_iface - span_pos * cols_count, mode="drop")
    )
    payload = interior_cols[:, jnp.minimum(slot_cell, cols_count - 1)]
    received = lax.all_to_all(payload, "span", split_axis=0, concat_axis=1, tiled=True)
    leaves = received[:, slot_index].reshape(
        plane_count, local_iface.shape[0], local_iface.shape[1]
    )
    levels = [leaves]
    current = leaves
    for blocks in (schur_one, schur_two, schur_three):
        paired = current[:, 0::2] + current[:, 1::2]
        current = jnp.einsum("mnij,mnj->mni", blocks, paired, precision=lax.Precision.HIGHEST)
        levels.append(current)
    partner = swapped(current, "dom", 0)
    top_value = jnp.einsum(
        "mnij,mnj->mni", schur_root, current + partner, precision=lax.Precision.HIGHEST
    )
    returned = jnp.einsum("mnji,mnj->mni", schur_root, top_value, precision=lax.Precision.HIGHEST)
    lowered = levels[3] - returned
    for blocks, below in ((schur_three, levels[2]), (schur_two, levels[1]), (schur_one, levels[0])):
        returned = jnp.einsum("mnji,mnj->mni", blocks, lowered, precision=lax.Precision.HIGHEST)
        lowered = below - jnp.repeat(returned, 2, axis=1)
    outgoing = (
        jnp.zeros((plane_count, span_count * slot_count), jnp.float32)
        .at[:, slot_index]
        .set(0.5 * lowered.reshape(plane_count, -1))
    )
    back_slots = lax.all_to_all(outgoing, "span", split_axis=1, concat_axis=0, tiled=True)
    corrected_cols = interior_cols.at[:, slot_cell].add(-back_slots, mode="drop")
    pressure_cols = jnp.dot(wave_table.T, corrected_cols, precision=lax.Precision.HIGHEST)
    pressure = lax.all_to_all(pressure_cols, "span", split_axis=0, concat_axis=1, tiled=True)
    corrected = scalar - stencil(pressure, span_vel, flux_weight, near_local)
    return (pressure, corrected)


def solution(mesh):
    placed = (
        P(("case", "span"), "dom"),
        P(("case", "span"), "dom"),
        P(None, "dom"),
        P(None, "dom"),
        P("dom"),
        P("dom", None),
        P("span", "dom", None, None),
        P("span", "dom", None, None),
        P("span", "dom", None, None),
        P("span", None, None, None),
    )
    return jax.shard_map(
        on_device,
        mesh=mesh,
        in_specs=placed,
        out_specs=(P(("case", "span"), "dom"), P(("case", "span"), "dom")),
        check_vma=False,
    )
```

```python
import math

import jax
import jax.numpy as jnp
from jax import lax
from jax.experimental import pallas as pl
from jax.experimental.pallas import tpu as pltpu
from jax.sharding import PartitionSpec as P

PLANES = 128
CELL_DOM = 512
HALO = 64


def extended(value, sides, width, wrap):
    for axis, dim in sides:
        count, length = (lax.axis_size(axis), value.shape[dim])
        up = [(i, (i + 1) % count) for i in range(count if wrap else count - 1)]
        down = [(j, i) for i, j in up]
        last = lax.slice_in_dim(value, length - width, length, axis=dim)
        initial = lax.slice_in_dim(value, 0, width, axis=dim)
        before = lax.ppermute(last, axis, up)
        after = lax.ppermute(initial, axis, down)
        value = jnp.concatenate([before, value, after], axis=dim)
    return value


def swapped(value, axis, distance):
    return lax.ppermute(value, axis, [(i, i ^ 1 << distance) for i in range(lax.axis_size(axis))])


def fourier_entry(wave_ids, plane_ids):
    middle = PLANES // 2
    wave_num = jnp.where(wave_ids <= middle, wave_ids, wave_ids - middle)
    phase_angle = (wave_num * plane_ids % PLANES).astype(jnp.float32) * (2.0 * math.pi / PLANES)
    at_edge = (wave_ids == 0) | (wave_ids == middle)
    weight_row = jnp.where(at_edge, math.sqrt(1.0 / PLANES), math.sqrt(2.0 / PLANES))
    return jnp.where(wave_ids <= middle, jnp.cos(phase_angle), jnp.sin(phase_angle)) * weight_row


def wave_shift(wave_ids):
    middle = PLANES // 2
    wave_num = jnp.where(wave_ids <= middle, wave_ids, wave_ids - middle).astype(jnp.float32)
    return (2.0 * jnp.sin(wave_num * (math.pi / PLANES))) ** 2


LANES = 128


def padded_rows(block):
    short = -block.shape[0] % 8
    if short == 0:
        return block
    return jnp.concatenate([block, jnp.zeros((short, block.shape[1]), block.dtype)], axis=0)


def flux_of(left, here, right, near, weight):
    rows = here.shape[0]
    turned = [pltpu.roll(padded_rows(piece), HALO, 1) for piece in (left, here, right)]
    full = turned[1].shape
    lane = lax.broadcasted_iota(jnp.int32, full, 1)
    low_part = jnp.where(lane < HALO, turned[0], turned[1])
    high_part = jnp.where(lane < HALO, turned[1], turned[2])
    total = jnp.zeros_like(here)
    for slot in range(near.shape[0]):
        index = jnp.broadcast_to(near[slot : slot + 1], full)
        within = index & (LANES - 1)
        low = jnp.take_along_axis(low_part, within, axis=1)
        high = jnp.take_along_axis(high_part, within, axis=1)
        picked = jnp.where(index < LANES, low, high)[:rows]
        total = total + weight[slot : slot + 1] * (picked - here)
    return total


def plane_difference(here, before, after):
    rows = here.shape[0]
    full = padded_rows(here)
    row = lax.broadcasted_iota(jnp.int32, full.shape, 0)
    ahead = jnp.where(row == rows - 1, after, pltpu.roll(full, full.shape[0] - 1, 0))
    behind = jnp.where(row == 0, before, pltpu.roll(full, 1, 0))
    return (ahead - behind)[:rows]


def stencil_kernel(start_ref, wide_ref, edge_ref, scalar_ref, vel_ref, weight_ref, near_ref, out_ref):
    start = start_ref[0]

    @pl.loop(0, out_ref.shape[1] // LANES)
    def _(block):
        at = pl.ds(pl.multiple_of(block * LANES, LANES), LANES)
        left, here, right = (
            wide_ref[:, pl.ds(pl.multiple_of((block + i) * LANES, LANES), LANES)] for i in range(3)
        )
        near = near_ref[:, at] - (start + block * LANES - HALO)
        flux = flux_of(left, here, right, near, weight_ref[:, at])
        change = plane_difference(here, edge_ref[0:1, at], edge_ref[1:2, at])
        out_ref[:, at] = scalar_ref[:, at] - (vel_ref[:, at] * 0.5 * change + flux)


def stepped(scalar, field, span_vel, flux_weight, neighbours, start):
    planes_ext = extended(field, (("span", 0),), 1, True)
    edge = jnp.concatenate([planes_ext[:1], planes_ext[-1:]], axis=0)
    wide = extended(field, (("dom", 1),), LANES, False)
    vmem = pl.BlockSpec(memory_space=pltpu.VMEM)
    return pl.pallas_call(
        stencil_kernel,
        out_shape=jax.ShapeDtypeStruct(field.shape, field.dtype),
        in_specs=[pl.BlockSpec(memory_space=pltpu.SMEM)] + [vmem] * 6,
        out_specs=vmem,
        compiler_params=pltpu.CompilerParams(vmem_limit_bytes=32 * 2**20),
    )(start.reshape(1), wide, edge, scalar, span_vel, flux_weight, neighbours)


def apply_table(table, block):
    return jnp.einsum("rp,pxc->rxc", table, block, precision=lax.Precision.HIGHEST)


def on_device(
    scalar,
    span_vel,
    flux_weight,
    neighbours,
    diagonal,
    interface,
    schur_one,
    schur_two,
    schur_three,
    schur_root,
):
    plane_count = scalar.shape[0]
    cell_count = scalar.shape[1]
    span_count = lax.axis_size("span")
    span_pos = lax.axis_index("span")
    cols_count = cell_count // span_count
    cell_start = lax.axis_index("dom") * cell_count
    source = stepped(scalar, scalar, span_vel, flux_weight, neighbours, cell_start)
    all_waves = jnp.arange(PLANES, dtype=jnp.int32)
    local_iface = interface - cell_start
    wave_table = fourier_entry(all_waves[:, None], all_waves[None, :])
    slot_count = min(cols_count, interface.shape[1] * max(1, cols_count // CELL_DOM))
    grouped = source.reshape(plane_count, span_count, cols_count)
    spectrum_cols = apply_table(
        wave_table, lax.all_to_all(grouped, "span", split_axis=1, concat_axis=0, tiled=True)
    ).reshape(PLANES, cols_count)
    diag_cols = lax.dynamic_slice_in_dim(diagonal, span_pos * cols_count, cols_count)
    interior_cols = spectrum_cols / (diag_cols[None, :] + wave_shift(all_waves)[:, None])
    flat_iface = local_iface.reshape(-1)
    owner = flat_iface // cols_count
    order = jnp.arange(flat_iface.shape[0], dtype=jnp.int32)
    earlier = (owner[:, None] == owner[None, :]) & (order[None, :] < order[:, None])
    ranks = jnp.sum(earlier.astype(jnp.int32), 1)
    slot_index = owner * slot_count + ranks
    owned = owner == span_pos
    slot_cell = (
        jnp.full((slot_count,), cols_count, jnp.int32)
        .at[jnp.where(owned, ranks, slot_count)]
        .set(flat_iface - span_pos * cols_count, mode="drop")
    )
    payload = interior_cols[:, jnp.minimum(slot_cell, cols_count - 1)]
    received = lax.all_to_all(payload, "span", split_axis=0, concat_axis=1, tiled=True)
    leaves = received[:, slot_index].reshape(
        plane_count, local_iface.shape[0], local_iface.shape[1]
    )
    levels = [leaves]
    current = leaves
    for blocks in (schur_one, schur_two, schur_three):
        paired = current[:, 0::2] + current[:, 1::2]
        current = jnp.einsum("mnij,mnj->mni", blocks, paired, precision=lax.Precision.HIGHEST)
        levels.append(current)
    partner = swapped(current, "dom", 0)
    top_value = jnp.einsum(
        "mnij,mnj->mni", schur_root, current + partner, precision=lax.Precision.HIGHEST
    )
    returned = jnp.einsum("mnji,mnj->mni", schur_root, top_value, precision=lax.Precision.HIGHEST)
    lowered = levels[3] - returned
    for blocks, below in ((schur_three, levels[2]), (schur_two, levels[1]), (schur_one, levels[0])):
        returned = jnp.einsum("mnji,mnj->mni", blocks, lowered, precision=lax.Precision.HIGHEST)
        lowered = below - jnp.repeat(returned, 2, axis=1)
    outgoing = (
        jnp.zeros((plane_count, span_count * slot_count), jnp.float32)
        .at[:, slot_index]
        .set(0.5 * lowered.reshape(plane_count, -1))
    )
    back_slots = lax.all_to_all(outgoing, "span", split_axis=1, concat_axis=0, tiled=True)
    corrected_cols = interior_cols.at[:, slot_cell].add(-back_slots, mode="drop")
    pressure_cols = jnp.dot(wave_table.T, corrected_cols, precision=lax.Precision.HIGHEST)
    pressure = lax.all_to_all(pressure_cols, "span", split_axis=0, concat_axis=1, tiled=True)
    corrected = stepped(scalar, pressure, span_vel, flux_weight, neighbours, cell_start)
    return (pressure, corrected)


def solution(mesh):
    placed = (
        P(("case", "span"), "dom"),
        P(("case", "span"), "dom"),
        P(None, "dom"),
        P(None, "dom"),
        P("dom"),
        P("dom", None),
        P("span", "dom", None, None),
        P("span", "dom", None, None),
        P("span", "dom", None, None),
        P("span", None, None, None),
    )
    return jax.shard_map(
        on_device,
        mesh=mesh,
        in_specs=placed,
        out_specs=(P(("case", "span"), "dom"), P(("case", "span"), "dom")),
        check_vma=False,
    )
```

```python
import functools
import math

import jax
import jax.numpy as jnp
from jax import lax
from jax.experimental import pallas as pl
from jax.experimental.pallas import tpu as pltpu
from jax.sharding import PartitionSpec as P

PLANES = 128
CELL_DOM = 512
HALO = 64


def extended(value, sides, width, wrap):
    for axis, dim in sides:
        count, length = (lax.axis_size(axis), value.shape[dim])
        up = [(i, (i + 1) % count) for i in range(count if wrap else count - 1)]
        down = [(j, i) for i, j in up]
        last = lax.slice_in_dim(value, length - width, length, axis=dim)
        initial = lax.slice_in_dim(value, 0, width, axis=dim)
        before = lax.ppermute(last, axis, up)
        after = lax.ppermute(initial, axis, down)
        value = jnp.concatenate([before, value, after], axis=dim)
    return value


def fourier_entry(wave_ids, plane_ids):
    middle = PLANES // 2
    wave_num = jnp.where(wave_ids <= middle, wave_ids, wave_ids - middle)
    phase_angle = (wave_num * plane_ids % PLANES).astype(jnp.float32) * (2.0 * math.pi / PLANES)
    at_edge = (wave_ids == 0) | (wave_ids == middle)
    weight_row = jnp.where(at_edge, math.sqrt(1.0 / PLANES), math.sqrt(2.0 / PLANES))
    return jnp.where(wave_ids <= middle, jnp.cos(phase_angle), jnp.sin(phase_angle)) * weight_row


def wave_shift(wave_ids):
    middle = PLANES // 2
    wave_num = jnp.where(wave_ids <= middle, wave_ids, wave_ids - middle).astype(jnp.float32)
    return (2.0 * jnp.sin(wave_num * (math.pi / PLANES))) ** 2


LANES = 128


def padded_rows(block):
    short = -block.shape[0] % 8
    if short == 0:
        return block
    return jnp.concatenate([block, jnp.zeros((short, block.shape[1]), block.dtype)], axis=0)


def flux_of(left, here, right, near, weight):
    rows = here.shape[0]
    turned = [pltpu.roll(padded_rows(piece), HALO, 1) for piece in (left, here, right)]
    full = turned[1].shape
    lane = lax.broadcasted_iota(jnp.int32, full, 1)
    low_part = jnp.where(lane < HALO, turned[0], turned[1])
    high_part = jnp.where(lane < HALO, turned[1], turned[2])
    total = jnp.zeros_like(here)
    for slot in range(near.shape[0]):
        index = jnp.broadcast_to(near[slot : slot + 1], full)
        within = index & (LANES - 1)
        low = jnp.take_along_axis(low_part, within, axis=1)
        high = jnp.take_along_axis(high_part, within, axis=1)
        picked = jnp.where(index < LANES, low, high)[:rows]
        total = total + weight[slot : slot + 1] * (picked - here)
    return total


def plane_difference(here, before, after):
    rows = here.shape[0]
    full = padded_rows(here)
    row = lax.broadcasted_iota(jnp.int32, full.shape, 0)
    ahead = jnp.where(row == rows - 1, after, pltpu.roll(full, full.shape[0] - 1, 0))
    behind = jnp.where(row == 0, before, pltpu.roll(full, 1, 0))
    return (ahead - behind)[:rows]


def stencil_kernel(start_ref, wide_ref, edge_ref, scalar_ref, vel_ref, weight_ref, near_ref, out_ref):
    start = start_ref[0]

    @pl.loop(0, out_ref.shape[1] // LANES)
    def _(block):
        at = pl.ds(pl.multiple_of(block * LANES, LANES), LANES)
        left, here, right = (
            wide_ref[:, pl.ds(pl.multiple_of((block + i) * LANES, LANES), LANES)] for i in range(3)
        )
        near = near_ref[:, at] - (start + block * LANES - HALO)
        flux = flux_of(left, here, right, near, weight_ref[:, at])
        change = plane_difference(here, edge_ref[0:1, at], edge_ref[1:2, at])
        out_ref[:, at] = scalar_ref[:, at] - (vel_ref[:, at] * 0.5 * change + flux)


def stepped(scalar, field, span_vel, flux_weight, neighbours, start):
    planes_ext = extended(field, (("span", 0),), 1, True)
    edge = jnp.concatenate([planes_ext[:1], planes_ext[-1:]], axis=0)
    wide = extended(field, (("dom", 1),), LANES, False)
    vmem = pl.BlockSpec(memory_space=pltpu.VMEM)
    return pl.pallas_call(
        stencil_kernel,
        out_shape=jax.ShapeDtypeStruct(field.shape, field.dtype),
        in_specs=[pl.BlockSpec(memory_space=pltpu.SMEM)] + [vmem] * 6,
        out_specs=vmem,
        compiler_params=pltpu.CompilerParams(vmem_limit_bytes=32 * 2**20),
    )(start.reshape(1), wide, edge, scalar, span_vel, flux_weight, neighbours)


def exact_dot(left, right, dims):
    return lax.dot_general(
        left, right, (dims, ((), ())), precision=lax.Precision.HIGHEST, preferred_element_type=jnp.float32
    )


def row_product(row, matrix, dim):
    rows = jnp.broadcast_to(row, (8, row.shape[1]))
    high = rows.astype(jnp.bfloat16).astype(jnp.float32)
    both = jnp.concatenate([high, rows - high], axis=0).astype(jnp.bfloat16)
    coarse = matrix.astype(jnp.bfloat16)
    fine = (matrix - coarse.astype(jnp.float32)).astype(jnp.bfloat16)
    dims = (((1,), (dim,)), ((), ()))
    main = lax.dot_general(both, coarse, dims, preferred_element_type=jnp.float32)
    rest = lax.dot_general(both, fine, dims, preferred_element_type=jnp.float32)
    return main[0:1] + (main[8:9] + (rest[0:1] + rest[8:9]))


def climb(below, blocks, above):
    @pl.loop(0, blocks.shape[0], unroll=4)
    def _(wave):
        at = pl.ds(wave, 1)
        for node in range(blocks.shape[1]):
            pair = below[2 * node, at, :] + below[2 * node + 1, at, :]
            above[node, at, :] = row_product(pair, blocks[wave, node], 1)


def descend(below, blocks, lowered, result):
    @pl.loop(0, blocks.shape[0], unroll=4)
    def _(wave):
        at = pl.ds(wave, 1)
        for node in range(blocks.shape[1]):
            returned = row_product(lowered[node, at, :], blocks[wave, node], 0)
            for child in (2 * node, 2 * node + 1):
                result[child, at, :] = below[child, at, :] - returned


def spectral_kernel(
    span_count, source_ref, table_ref, diag_ref, shift_ref, iface_ref, one_hbm, two_hbm, three_hbm, root_hbm, out_ref,
    one, two, three, root, source_in, leaf_out, leaf_in, press_out, press_in, back_in, fix_out, fix_in,
    s0, s1, s2, s3, g0, g1, g2, g3, partner, load_sem, send_sem, recv_sem, swap_sem,
):
    planes, cells = source_ref.shape
    cols = cells // span_count
    domains, slots = iface_ref.shape
    shares = span_count // domains
    me = lax.axis_index("span")
    half = lax.axis_index("dom")
    barrier = pltpu.get_barrier_semaphore()
    kind = pl.DeviceIdType.MESH
    loads = [
        pltpu.make_async_copy(src, dst, load_sem.at[i])
        for i, (src, dst) in enumerate(((one_hbm, one), (two_hbm, two), (three_hbm, three), (root_hbm, root)))
    ]
    for load in loads:
        load.start()
    peers = [lax.rem(me + i, span_count) for i in range(1, span_count)]
    for peer in peers:
        pl.semaphore_signal(barrier, inc=1, device_id={"span": peer}, device_id_type=kind)
    pl.semaphore_signal(barrier, inc=1, device_id={"dom": 1 - half}, device_id_type=kind)
    pl.semaphore_wait(barrier, span_count)

    def exchange(phase, pick, landing):
        copies = []
        for i, peer in enumerate(peers):
            copies.append(
                pltpu.make_async_remote_copy(
                    src_ref=pick(peer),
                    dst_ref=landing.at[me],
                    send_sem=send_sem.at[phase, i],
                    recv_sem=recv_sem.at[phase, i],
                    device_id={"span": peer},
                    device_id_type=kind,
                )
            )
            copies[-1].start()
        return copies

    def arrived(copies):
        for copy in copies:
            copy.wait_recv()

    def columns_of(owner):
        return pl.ds(pl.multiple_of(owner * cols, LANES), cols)

    def hot(domain_row, first):
        cell = lax.broadcasted_iota(jnp.int32, (cols, slots), 0) + first
        return (cell == domain_row).astype(jnp.float32)

    sent = exchange(0, lambda peer: source_ref.at[:, columns_of(peer)], source_in)
    source_in[me] = source_ref[:, columns_of(me)]
    own_domain = lax.div(me, shares)
    own_hot = hot(iface_ref[pl.ds(own_domain, 1), :], half * cells + me * cols)
    divisor = diag_ref[:, columns_of(me)] + shift_ref[...]
    arrived(sent)
    block = source_in[...].reshape(span_count * planes, cols)
    interior = exact_dot(table_ref[...], block, ((1,), (0,))) / divisor
    leaf_out[...] = exact_dot(interior, own_hot, ((1,), (0,))).reshape(leaf_out.shape)
    leaves = exchange(1, lambda peer: leaf_out.at[peer], leaf_in)
    leaf_in[me] = leaf_out[me]
    press_out[...] = exact_dot(table_ref[...], interior, ((0,), (0,))).reshape(press_out.shape)
    for load in loads:
        load.wait()
    arrived(leaves)
    pressed = exchange(2, lambda peer: press_out.at[peer], press_in)
    press_in[me] = press_out[me]
    for domain in range(domains):
        s0[domain] = sum(leaf_in[domain * shares + i] for i in range(shares))
    climb(s0, one, s1)
    climb(s1, two, s2)
    climb(s2, three, s3)
    swap = pltpu.make_async_remote_copy(
        src_ref=s3,
        dst_ref=partner,
        send_sem=swap_sem.at[0],
        recv_sem=swap_sem.at[1],
        device_id={"dom": 1 - half},
        device_id_type=kind,
    )
    swap.start()
    swap.wait_recv()

    @pl.loop(0, planes, unroll=4)
    def _(wave):
        at = pl.ds(wave, 1)
        top = row_product(s3[0, at, :] + partner[0, at, :], root[wave, 0], 1)
        g3[0, at, :] = s3[0, at, :] - row_product(top, root[wave, 0], 0)

    descend(s2, three, g3, g2)
    descend(s1, two, g2, g1)
    descend(s0, one, g1, g0)
    backs = exchange(3, lambda peer: g0.at[lax.div(peer, shares)], back_in)
    back_in[me] = g0[own_domain]
    arrived(backs)
    back = back_in[...].reshape(span_count * planes, slots)
    fix_out[...] = exact_dot(table_ref[...], 0.5 * back, ((0,), (0,))).reshape(fix_out.shape)
    fixes = exchange(4, lambda peer: fix_out.at[peer], fix_in)
    fix_in[me] = fix_out[me]
    arrived(pressed)
    arrived(fixes)

    @pl.loop(0, span_count)
    def _(owner):
        domain = lax.div(owner, shares)
        where = hot(iface_ref[pl.ds(domain, 1), :], half * cells + owner * cols)
        added = exact_dot(fix_in[domain * shares], where, ((1,), (1,)))
        out_ref[:, columns_of(owner)] = press_in[owner] - added

    for copies in (sent, leaves, pressed, backs, fixes, [swap]):
        for copy in copies:
            copy.wait_send()


def projected(source, table, diagonal, shift, interface, blocks, span_count):
    planes, cells = source.shape
    cols = cells // span_count
    domains, slots = interface.shape
    vmem = pl.BlockSpec(memory_space=pltpu.VMEM)
    hbm = pl.BlockSpec(memory_space=pl.ANY)
    wide, narrow = (span_count, planes, cols), (span_count, planes, slots)
    nodes = [domains >> level for level in range(4)]
    levels = [(node, planes, slots) for node in nodes]
    shapes = [wide, narrow, narrow, wide, wide, narrow, narrow, narrow] + levels + levels + [levels[3]]
    return pl.pallas_call(
        functools.partial(spectral_kernel, span_count),
        out_shape=jax.ShapeDtypeStruct(source.shape, source.dtype),
        in_specs=[vmem] * 5 + [hbm] * 4,
        out_specs=vmem,
        scratch_shapes=[pltpu.VMEM(block.shape, block.dtype) for block in blocks]
        + [pltpu.VMEM(shape, jnp.float32) for shape in shapes]
        + [
            pltpu.SemaphoreType.DMA((4,)),
            pltpu.SemaphoreType.DMA((5, span_count - 1)),
            pltpu.SemaphoreType.DMA((5, span_count - 1)),
            pltpu.SemaphoreType.DMA((2,)),
        ],
        compiler_params=pltpu.CompilerParams(
            collective_id=0, has_side_effects=True, vmem_limit_bytes=40 * 2**20
        ),
    )(source, table, diagonal, shift, interface, *blocks)


def on_device(
    scalar,
    span_vel,
    flux_weight,
    neighbours,
    diagonal,
    interface,
    schur_one,
    schur_two,
    schur_three,
    schur_root,
):
    cell_start = lax.axis_index("dom") * scalar.shape[1]
    waves = jnp.arange(PLANES, dtype=jnp.int32)
    table = fourier_entry(waves[:, None], waves[None, :])
    shift = wave_shift(waves)[:, None]
    source = stepped(scalar, scalar, span_vel, flux_weight, neighbours, cell_start)
    blocks = (schur_one, schur_two, schur_three, schur_root)
    pressure = projected(
        source, table, diagonal[None, :], shift, interface, blocks, lax.axis_size("span")
    )
    corrected = stepped(scalar, pressure, span_vel, flux_weight, neighbours, cell_start)
    return (pressure, corrected)


def solution(mesh):
    placed = (
        P(("case", "span"), "dom"),
        P(("case", "span"), "dom"),
        P(None, "dom"),
        P(None, "dom"),
        P("dom"),
        P("dom", None),
        P("span", "dom", None, None),
        P("span", "dom", None, None),
        P("span", "dom", None, None),
        P("span", None, None, None),
    )
    return jax.shard_map(
        on_device,
        mesh=mesh,
        in_specs=placed,
        out_specs=(P(("case", "span"), "dom"), P(("case", "span"), "dom")),
        check_vma=False,
    )
```

```python
import functools
import math

import jax
import jax.numpy as jnp
from jax import lax
from jax.experimental import pallas as pl
from jax.experimental.pallas import tpu as pltpu
from jax.sharding import PartitionSpec as P

PLANES = 128
CELL_DOM = 512
HALO = 64


def fourier_entry(wave_ids, plane_ids):
    middle = PLANES // 2
    wave_num = jnp.where(wave_ids <= middle, wave_ids, wave_ids - middle)
    phase_angle = (wave_num * plane_ids % PLANES).astype(jnp.float32) * (2.0 * math.pi / PLANES)
    at_edge = (wave_ids == 0) | (wave_ids == middle)
    weight_row = jnp.where(at_edge, math.sqrt(1.0 / PLANES), math.sqrt(2.0 / PLANES))
    return jnp.where(wave_ids <= middle, jnp.cos(phase_angle), jnp.sin(phase_angle)) * weight_row


def wave_shift(wave_ids):
    middle = PLANES // 2
    wave_num = jnp.where(wave_ids <= middle, wave_ids, wave_ids - middle).astype(jnp.float32)
    return (2.0 * jnp.sin(wave_num * (math.pi / PLANES))) ** 2


LANES = 128


def padded_rows(block):
    short = -block.shape[0] % 8
    if short == 0:
        return block
    return jnp.concatenate([block, jnp.zeros((short, block.shape[1]), block.dtype)], axis=0)


def flux_of(left, here, right, near, weight):
    rows = here.shape[0]
    turned = [pltpu.roll(padded_rows(piece), HALO, 1) for piece in (left, here, right)]
    full = turned[1].shape
    lane = lax.broadcasted_iota(jnp.int32, full, 1)
    low_part = jnp.where(lane < HALO, turned[0], turned[1])
    high_part = jnp.where(lane < HALO, turned[1], turned[2])
    total = jnp.zeros_like(here)
    for slot in range(near.shape[0]):
        index = jnp.broadcast_to(near[slot : slot + 1], full)
        within = index & (LANES - 1)
        low = jnp.take_along_axis(low_part, within, axis=1)
        high = jnp.take_along_axis(high_part, within, axis=1)
        picked = jnp.where(index < LANES, low, high)[:rows]
        total = total + weight[slot : slot + 1] * (picked - here)
    return total


def plane_difference(here, before, after):
    rows = here.shape[0]
    full = padded_rows(here)
    row = lax.broadcasted_iota(jnp.int32, full.shape, 0)
    ahead = jnp.where(row == rows - 1, after, pltpu.roll(full, full.shape[0] - 1, 0))
    behind = jnp.where(row == 0, before, pltpu.roll(full, 1, 0))
    return (ahead - behind)[:rows]


def stepped(start, wide, edge, scalar_ref, vel_ref, weight_ref, near_ref, out_ref):
    @pl.loop(0, out_ref.shape[1] // LANES)
    def _(block):
        at = pl.ds(pl.multiple_of(block * LANES, LANES), LANES)
        left, here, right = (
            wide[:, pl.ds(pl.multiple_of((block + i) * LANES, LANES), LANES)] for i in range(3)
        )
        near = near_ref[:, at] - (start + block * LANES - HALO)
        flux = flux_of(left, here, right, near, weight_ref[:, at])
        change = plane_difference(here, edge[0:1, at], edge[8:9, at])
        out_ref[:, at] = scalar_ref[:, at] - (vel_ref[:, at] * 0.5 * change + flux)


def exact_dot(left, right, dims):
    return lax.dot_general(
        left, right, (dims, ((), ())), precision=lax.Precision.HIGHEST, preferred_element_type=jnp.float32
    )


def row_product(row, matrix, dim):
    rows = jnp.broadcast_to(row, (8, row.shape[1]))
    high = rows.astype(jnp.bfloat16).astype(jnp.float32)
    both = jnp.concatenate([high, rows - high], axis=0).astype(jnp.bfloat16)
    coarse = matrix.astype(jnp.bfloat16)
    fine = (matrix - coarse.astype(jnp.float32)).astype(jnp.bfloat16)
    dims = (((1,), (dim,)), ((), ()))
    main = lax.dot_general(both, coarse, dims, preferred_element_type=jnp.float32)
    rest = lax.dot_general(both, fine, dims, preferred_element_type=jnp.float32)
    return main[0:1] + (main[8:9] + (rest[0:1] + rest[8:9]))


def climb(below, blocks, above):
    @pl.loop(0, blocks.shape[0], unroll=4)
    def _(wave):
        at = pl.ds(wave, 1)
        for node in range(blocks.shape[1]):
            pair = below[2 * node, at, :] + below[2 * node + 1, at, :]
            above[node, at, :] = row_product(pair, blocks[wave, node], 1)


def descend(below, blocks, lowered, result):
    @pl.loop(0, blocks.shape[0], unroll=4)
    def _(wave):
        at = pl.ds(wave, 1)
        for node in range(blocks.shape[1]):
            returned = row_product(lowered[node, at, :], blocks[wave, node], 0)
            for child in (2 * node, 2 * node + 1):
                result[child, at, :] = below[child, at, :] - returned


def spectral_kernel(
    span_count, scalar_ref, vel_ref, weight_ref, near_ref, table_ref, diag_ref, shift_ref, iface_ref,
    one_hbm, two_hbm, three_hbm, root_hbm, out_ref, corrected_ref, source_ref, wide, later, edge, later_edge,
    one, two, three, root, source_in, leaf_out, leaf_in, press_out, press_in, back_in, fix_out, fix_in,
    s0, s1, s2, s3, g0, g1, g2, g3, partner, load_sem, send_sem, recv_sem, swap_sem, halo_sem,
):
    planes, cells = scalar_ref.shape
    cols = cells // span_count
    domains, slots = iface_ref.shape
    shares = span_count // domains
    me = lax.axis_index("span")
    half = lax.axis_index("dom")
    barrier = pltpu.get_barrier_semaphore()
    kind = pl.DeviceIdType.MESH
    loads = [
        pltpu.make_async_copy(src, dst, load_sem.at[i])
        for i, (src, dst) in enumerate(((one_hbm, one), (two_hbm, two), (three_hbm, three), (root_hbm, root)))
    ]
    for load in loads:
        load.start()
    for field in (wide, later):
        for place in (0, LANES + cells):
            field[:, place : place + LANES] = jnp.zeros((planes, LANES), jnp.float32)
    wide[:, LANES : LANES + cells] = scalar_ref[...]
    peers = [lax.rem(me + i, span_count) for i in range(1, span_count)]
    for peer in peers:
        pl.semaphore_signal(barrier, inc=1, device_id={"span": peer}, device_id_type=kind)
    pl.semaphore_signal(barrier, inc=1, device_id={"dom": 1 - half}, device_id_type=kind)
    pl.semaphore_wait(barrier, span_count)

    def halo(phase, field, rows):
        own = pl.ds(LANES, cells)
        block_from = pl.ds(pl.multiple_of((1 - half) * (cells - LANES) + LANES, LANES), LANES)
        block_to = pl.ds(pl.multiple_of(half * (cells + LANES), LANES), LANES)
        plan = (
            (field.at[pl.ds(planes - 1, 1), own], rows.at[pl.ds(0, 1)], {"span": lax.rem(me + 1, span_count)}),
            (field.at[pl.ds(0, 1), own], rows.at[pl.ds(8, 1)], {"span": lax.rem(me + span_count - 1, span_count)}),
            (field.at[:, block_from], field.at[:, block_to], {"dom": 1 - half}),
        )
        copies = [
            pltpu.make_async_remote_copy(
                src_ref=source,
                dst_ref=target,
                send_sem=halo_sem.at[phase, 0, i],
                recv_sem=halo_sem.at[phase, 1, i],
                device_id=device,
                device_id_type=kind,
            )
            for i, (source, target, device) in enumerate(plan)
        ]
        for copy in copies:
            copy.start()
        for copy in copies:
            copy.wait_send()
        for copy in copies:
            copy.wait_recv()

    def exchange(phase, pick, landing):
        copies = []
        for i, peer in enumerate(peers):
            copies.append(
                pltpu.make_async_remote_copy(
                    src_ref=pick(peer),
                    dst_ref=landing.at[me],
                    send_sem=send_sem.at[phase, i],
                    recv_sem=recv_sem.at[phase, i],
                    device_id={"span": peer},
                    device_id_type=kind,
                )
            )
            copies[-1].start()
        return copies

    def arrived(copies):
        for copy in copies:
            copy.wait_recv()

    def columns_of(owner):
        return pl.ds(pl.multiple_of(owner * cols, LANES), cols)

    def hot(domain_row, first):
        cell = lax.broadcasted_iota(jnp.int32, (cols, slots), 0) + first
        return (cell == domain_row).astype(jnp.float32)

    constants = (scalar_ref, vel_ref, weight_ref, near_ref)
    halo(0, wide, edge)
    stepped(half * cells, wide, edge, *constants, source_ref)
    sent = exchange(0, lambda peer: source_ref.at[:, columns_of(peer)], source_in)
    source_in[me] = source_ref[:, columns_of(me)]
    own_domain = lax.div(me, shares)
    own_hot = hot(iface_ref[pl.ds(own_domain, 1), :], half * cells + me * cols)
    divisor = diag_ref[:, columns_of(me)] + shift_ref[...]
    arrived(sent)
    block = source_in[...].reshape(span_count * planes, cols)
    interior = exact_dot(table_ref[...], block, ((1,), (0,))) / divisor
    leaf_out[...] = exact_dot(interior, own_hot, ((1,), (0,))).reshape(leaf_out.shape)
    leaves = exchange(1, lambda peer: leaf_out.at[peer], leaf_in)
    leaf_in[me] = leaf_out[me]
    press_out[...] = exact_dot(table_ref[...], interior, ((0,), (0,))).reshape(press_out.shape)
    for load in loads:
        load.wait()
    arrived(leaves)
    pressed = exchange(2, lambda peer: press_out.at[peer], press_in)
    press_in[me] = press_out[me]
    for domain in range(domains):
        s0[domain] = sum(leaf_in[domain * shares + i] for i in range(shares))
    climb(s0, one, s1)
    climb(s1, two, s2)
    climb(s2, three, s3)
    swap = pltpu.make_async_remote_copy(
        src_ref=s3,
        dst_ref=partner,
        send_sem=swap_sem.at[0],
        recv_sem=swap_sem.at[1],
        device_id={"dom": 1 - half},
        device_id_type=kind,
    )
    swap.start()
    swap.wait_recv()

    @pl.loop(0, planes, unroll=4)
    def _(wave):
        at = pl.ds(wave, 1)
        top = row_product(s3[0, at, :] + partner[0, at, :], root[wave, 0], 1)
        g3[0, at, :] = s3[0, at, :] - row_product(top, root[wave, 0], 0)

    descend(s2, three, g3, g2)
    descend(s1, two, g2, g1)
    descend(s0, one, g1, g0)
    backs = exchange(3, lambda peer: g0.at[lax.div(peer, shares)], back_in)
    back_in[me] = g0[own_domain]
    arrived(backs)
    back = back_in[...].reshape(span_count * planes, slots)
    fix_out[...] = exact_dot(table_ref[...], 0.5 * back, ((0,), (0,))).reshape(fix_out.shape)
    fixes = exchange(4, lambda peer: fix_out.at[peer], fix_in)
    fix_in[me] = fix_out[me]
    arrived(pressed)
    arrived(fixes)

    @pl.loop(0, span_count)
    def _(owner):
        domain = lax.div(owner, shares)
        where = hot(iface_ref[pl.ds(domain, 1), :], half * cells + owner * cols)
        added = exact_dot(fix_in[domain * shares], where, ((1,), (1,)))
        value = press_in[owner] - added
        out_ref[:, columns_of(owner)] = value
        later[:, pl.ds(pl.multiple_of(owner * cols + LANES, LANES), cols)] = value

    halo(1, later, later_edge)
    stepped(half * cells, later, later_edge, *constants, corrected_ref)

    for copies in (sent, leaves, pressed, backs, fixes, [swap]):
        for copy in copies:
            copy.wait_send()


def projected(scalar, vel, weight, near, table, diagonal, shift, interface, blocks, span_count):
    planes, cells = scalar.shape
    cols = cells // span_count
    domains, slots = interface.shape
    vmem = pl.BlockSpec(memory_space=pltpu.VMEM)
    hbm = pl.BlockSpec(memory_space=pl.ANY)
    wide, narrow = (span_count, planes, cols), (span_count, planes, slots)
    nodes = [domains >> level for level in range(4)]
    levels = [(node, planes, slots) for node in nodes]
    fields = [(planes, cells)] + [(planes, cells + 2 * LANES)] * 2 + [(16, cells)] * 2
    shapes = [wide, narrow, narrow, wide, wide, narrow, narrow, narrow] + levels + levels + [levels[3]]
    return pl.pallas_call(
        functools.partial(spectral_kernel, span_count),
        out_shape=(jax.ShapeDtypeStruct(scalar.shape, scalar.dtype),) * 2,
        in_specs=[vmem] * 8 + [hbm] * 4,
        out_specs=(vmem, vmem),
        scratch_shapes=[pltpu.VMEM(shape, jnp.float32) for shape in fields]
        + [pltpu.VMEM(block.shape, block.dtype) for block in blocks]
        + [pltpu.VMEM(shape, jnp.float32) for shape in shapes]
        + [
            pltpu.SemaphoreType.DMA((4,)),
            pltpu.SemaphoreType.DMA((5, span_count - 1)),
            pltpu.SemaphoreType.DMA((5, span_count - 1)),
            pltpu.SemaphoreType.DMA((2,)),
            pltpu.SemaphoreType.DMA((2, 2, 3)),
        ],
        compiler_params=pltpu.CompilerParams(
            collective_id=0, has_side_effects=True, vmem_limit_bytes=40 * 2**20
        ),
    )(scalar, vel, weight, near, table, diagonal, shift, interface, *blocks)


def on_device(
    scalar,
    span_vel,
    flux_weight,
    neighbours,
    diagonal,
    interface,
    schur_one,
    schur_two,
    schur_three,
    schur_root,
):
    waves = jnp.arange(PLANES, dtype=jnp.int32)
    table = fourier_entry(waves[:, None], waves[None, :])
    shift = wave_shift(waves)[:, None]
    blocks = (schur_one, schur_two, schur_three, schur_root)
    return projected(
        scalar,
        span_vel,
        flux_weight,
        neighbours,
        table,
        diagonal[None, :],
        shift,
        interface,
        blocks,
        lax.axis_size("span"),
    )


def solution(mesh):
    placed = (
        P(("case", "span"), "dom"),
        P(("case", "span"), "dom"),
        P(None, "dom"),
        P(None, "dom"),
        P("dom"),
        P("dom", None),
        P("span", "dom", None, None),
        P("span", "dom", None, None),
        P("span", "dom", None, None),
        P("span", None, None, None),
    )
    return jax.shard_map(
        on_device,
        mesh=mesh,
        in_specs=placed,
        out_specs=(P(("case", "span"), "dom"), P(("case", "span"), "dom")),
        check_vma=False,
    )
```

```python
import functools
import math

import jax
import jax.numpy as jnp
from jax import lax
from jax.experimental import pallas as pl
from jax.experimental.pallas import tpu as pltpu
from jax.sharding import PartitionSpec as P

PLANES = 128
CELL_DOM = 512
HALO = 64


def fourier_entry(wave_ids, plane_ids):
    middle = PLANES // 2
    wave_num = jnp.where(wave_ids <= middle, wave_ids, wave_ids - middle)
    phase_angle = (wave_num * plane_ids % PLANES).astype(jnp.float32) * (2.0 * math.pi / PLANES)
    at_edge = (wave_ids == 0) | (wave_ids == middle)
    weight_row = jnp.where(at_edge, math.sqrt(1.0 / PLANES), math.sqrt(2.0 / PLANES))
    return jnp.where(wave_ids <= middle, jnp.cos(phase_angle), jnp.sin(phase_angle)) * weight_row


def wave_shift(wave_ids):
    middle = PLANES // 2
    wave_num = jnp.where(wave_ids <= middle, wave_ids, wave_ids - middle).astype(jnp.float32)
    return (2.0 * jnp.sin(wave_num * (math.pi / PLANES))) ** 2


LANES = 128


def padded_rows(block):
    short = -block.shape[0] % 8
    if short == 0:
        return block
    return jnp.concatenate([block, jnp.zeros((short, block.shape[1]), block.dtype)], axis=0)


def flux_of(left, here, right, near, weight):
    rows = here.shape[0]
    turned = [pltpu.roll(padded_rows(piece), HALO, 1) for piece in (left, here, right)]
    full = turned[1].shape
    lane = lax.broadcasted_iota(jnp.int32, full, 1)
    low_part = jnp.where(lane < HALO, turned[0], turned[1])
    high_part = jnp.where(lane < HALO, turned[1], turned[2])
    total = jnp.zeros_like(here)
    for slot in range(near.shape[0]):
        index = jnp.broadcast_to(near[slot : slot + 1], full)
        within = index & (LANES - 1)
        low = jnp.take_along_axis(low_part, within, axis=1)
        high = jnp.take_along_axis(high_part, within, axis=1)
        picked = jnp.where(index < LANES, low, high)[:rows]
        total = total + weight[slot : slot + 1] * (picked - here)
    return total


def plane_difference(here, before, after):
    rows = here.shape[0]
    full = padded_rows(here)
    row = lax.broadcasted_iota(jnp.int32, full.shape, 0)
    ahead = jnp.where(row == rows - 1, after, pltpu.roll(full, full.shape[0] - 1, 0))
    behind = jnp.where(row == 0, before, pltpu.roll(full, 1, 0))
    return (ahead - behind)[:rows]


def stepped(start, wide, edge, scalar_ref, vel_ref, weight_ref, near_ref, out_ref):
    @pl.loop(0, out_ref.shape[1] // LANES, unroll=4)
    def _(block):
        at = pl.ds(pl.multiple_of(block * LANES, LANES), LANES)
        left, here, right = (
            wide[:, pl.ds(pl.multiple_of((block + i) * LANES, LANES), LANES)] for i in range(3)
        )
        near = near_ref[:, at] - (start + block * LANES - HALO)
        flux = flux_of(left, here, right, near, weight_ref[:, at])
        change = plane_difference(here, edge[0:1, at], edge[8:9, at])
        out_ref[:, at] = scalar_ref[:, at] - (vel_ref[:, at] * 0.5 * change + flux)


def exact_dot(left, right, dims):
    return lax.dot_general(
        left, right, (dims, ((), ())), precision=lax.Precision.HIGHEST, preferred_element_type=jnp.float32
    )


def row_product(row, matrix, dim):
    rows = jnp.broadcast_to(row, (8, row.shape[1]))
    high = rows.astype(jnp.bfloat16).astype(jnp.float32)
    both = jnp.concatenate([high, rows - high], axis=0).astype(jnp.bfloat16)
    coarse = matrix.astype(jnp.bfloat16)
    fine = (matrix - coarse.astype(jnp.float32)).astype(jnp.bfloat16)
    dims = (((1,), (dim,)), ((), ()))
    main = lax.dot_general(both, coarse, dims, preferred_element_type=jnp.float32)
    rest = lax.dot_general(both, fine, dims, preferred_element_type=jnp.float32)
    return main[0:1] + (main[8:9] + (rest[0:1] + rest[8:9]))


def climb(below, blocks, above):
    @pl.loop(0, blocks.shape[0], unroll=4)
    def _(wave):
        at = pl.ds(wave, 1)
        for node in range(blocks.shape[1]):
            pair = below[2 * node, at, :] + below[2 * node + 1, at, :]
            above[node, at, :] = row_product(pair, blocks[wave, node], 1)


def descend(below, blocks, lowered, result):
    @pl.loop(0, blocks.shape[0], unroll=4)
    def _(wave):
        at = pl.ds(wave, 1)
        for node in range(blocks.shape[1]):
            returned = row_product(lowered[node, at, :], blocks[wave, node], 0)
            for child in (2 * node, 2 * node + 1):
                result[child, at, :] = below[child, at, :] - returned


def spectral_kernel(
    span_count, scalar_ref, vel_ref, weight_ref, near_ref, table_ref, diag_ref, shift_ref, iface_ref,
    one_hbm, two_hbm, three_hbm, root_hbm, out_ref, corrected_ref, source_ref, wide, later, edge, later_edge,
    one, two, three, root, source_in, leaf_out, leaf_in, press_out, press_in, back_in, fix_out, fix_in,
    s0, s1, s2, s3, g0, g1, g2, g3, partner, load_sem, send_sem, recv_sem, swap_sem, halo_sem,
):
    planes, cells = scalar_ref.shape
    cols = cells // span_count
    domains, slots = iface_ref.shape
    shares = span_count // domains
    me = lax.axis_index("span")
    half = lax.axis_index("dom")
    barrier = pltpu.get_barrier_semaphore()
    kind = pl.DeviceIdType.MESH
    loads = [
        pltpu.make_async_copy(src, dst, load_sem.at[i])
        for i, (src, dst) in enumerate(((one_hbm, one), (two_hbm, two), (three_hbm, three), (root_hbm, root)))
    ]
    for load in loads:
        load.start()
    for field in (wide, later):
        for place in (0, LANES + cells):
            field[:, place : place + LANES] = jnp.zeros((planes, LANES), jnp.float32)
    wide[:, LANES : LANES + cells] = scalar_ref[...]
    peers = [lax.rem(me + i, span_count) for i in range(1, span_count)]
    for peer in peers:
        pl.semaphore_signal(barrier, inc=1, device_id={"span": peer}, device_id_type=kind)
    pl.semaphore_signal(barrier, inc=1, device_id={"dom": 1 - half}, device_id_type=kind)
    pl.semaphore_wait(barrier, span_count)

    def halo(phase, field, rows):
        own = pl.ds(LANES, cells)
        block_from = pl.ds(pl.multiple_of((1 - half) * (cells - LANES) + LANES, LANES), LANES)
        block_to = pl.ds(pl.multiple_of(half * (cells + LANES), LANES), LANES)
        plan = (
            (field.at[pl.ds(planes - 1, 1), own], rows.at[pl.ds(0, 1)], {"span": lax.rem(me + 1, span_count)}),
            (field.at[pl.ds(0, 1), own], rows.at[pl.ds(8, 1)], {"span": lax.rem(me + span_count - 1, span_count)}),
            (field.at[:, block_from], field.at[:, block_to], {"dom": 1 - half}),
        )
        copies = [
            pltpu.make_async_remote_copy(
                src_ref=source,
                dst_ref=target,
                send_sem=halo_sem.at[phase, 0, i],
                recv_sem=halo_sem.at[phase, 1, i],
                device_id=device,
                device_id_type=kind,
            )
            for i, (source, target, device) in enumerate(plan)
        ]
        for copy in copies:
            copy.start()
        for copy in copies:
            copy.wait_send()
        for copy in copies:
            copy.wait_recv()

    def exchange(phase, pick, landing):
        copies = []
        for i, peer in enumerate(peers):
            copies.append(
                pltpu.make_async_remote_copy(
                    src_ref=pick(peer),
                    dst_ref=landing.at[me],
                    send_sem=send_sem.at[phase, i],
                    recv_sem=recv_sem.at[phase, i],
                    device_id={"span": peer},
                    device_id_type=kind,
                )
            )
            copies[-1].start()
        return copies

    def arrived(copies):
        for copy in copies:
            copy.wait_recv()

    def columns_of(owner):
        return pl.ds(pl.multiple_of(owner * cols, LANES), cols)

    def hot(domain_row, first):
        cell = lax.broadcasted_iota(jnp.int32, (cols, slots), 0) + first
        return (cell == domain_row).astype(jnp.float32)

    constants = (scalar_ref, vel_ref, weight_ref, near_ref)
    halo(0, wide, edge)
    stepped(half * cells, wide, edge, *constants, source_ref)
    sent = exchange(0, lambda peer: source_ref.at[:, columns_of(peer)], source_in)
    source_in[me] = source_ref[:, columns_of(me)]
    own_domain = lax.div(me, shares)
    own_hot = hot(iface_ref[pl.ds(own_domain, 1), :], half * cells + me * cols)
    divisor = diag_ref[:, columns_of(me)] + shift_ref[...]
    arrived(sent)
    block = source_in[...].reshape(span_count * planes, cols)
    interior = exact_dot(table_ref[...], block, ((1,), (0,))) / divisor
    leaf_out[...] = exact_dot(interior, own_hot, ((1,), (0,))).reshape(leaf_out.shape)
    leaves = exchange(1, lambda peer: leaf_out.at[peer], leaf_in)
    leaf_in[me] = leaf_out[me]
    press_out[...] = exact_dot(table_ref[...], interior, ((0,), (0,))).reshape(press_out.shape)
    for load in loads:
        load.wait()
    arrived(leaves)
    pressed = exchange(2, lambda peer: press_out.at[peer], press_in)
    press_in[me] = press_out[me]
    for domain in range(domains):
        s0[domain] = sum(leaf_in[domain * shares + i] for i in range(shares))
    climb(s0, one, s1)
    climb(s1, two, s2)
    climb(s2, three, s3)
    swap = pltpu.make_async_remote_copy(
        src_ref=s3,
        dst_ref=partner,
        send_sem=swap_sem.at[0],
        recv_sem=swap_sem.at[1],
        device_id={"dom": 1 - half},
        device_id_type=kind,
    )
    swap.start()
    swap.wait_recv()

    @pl.loop(0, planes, unroll=4)
    def _(wave):
        at = pl.ds(wave, 1)
        top = row_product(s3[0, at, :] + partner[0, at, :], root[wave, 0], 1)
        g3[0, at, :] = s3[0, at, :] - row_product(top, root[wave, 0], 0)

    descend(s2, three, g3, g2)
    descend(s1, two, g2, g1)
    descend(s0, one, g1, g0)
    backs = exchange(3, lambda peer: g0.at[lax.div(peer, shares)], back_in)
    back_in[me] = g0[own_domain]
    arrived(backs)
    back = back_in[...].reshape(span_count * planes, slots)
    fix_out[...] = exact_dot(table_ref[...], 0.5 * back, ((0,), (0,))).reshape(fix_out.shape)
    fixes = exchange(4, lambda peer: fix_out.at[peer], fix_in)
    fix_in[me] = fix_out[me]
    arrived(pressed)
    arrived(fixes)

    @pl.loop(0, span_count)
    def _(owner):
        domain = lax.div(owner, shares)
        where = hot(iface_ref[pl.ds(domain, 1), :], half * cells + owner * cols)
        added = exact_dot(fix_in[domain * shares], where, ((1,), (1,)))
        value = press_in[owner] - added
        out_ref[:, columns_of(owner)] = value
        later[:, pl.ds(pl.multiple_of(owner * cols + LANES, LANES), cols)] = value

    halo(1, later, later_edge)
    stepped(half * cells, later, later_edge, *constants, corrected_ref)

    for copies in (sent, leaves, pressed, backs, fixes, [swap]):
        for copy in copies:
            copy.wait_send()


def projected(scalar, vel, weight, near, table, diagonal, shift, interface, blocks, span_count):
    planes, cells = scalar.shape
    cols = cells // span_count
    domains, slots = interface.shape
    vmem = pl.BlockSpec(memory_space=pltpu.VMEM)
    hbm = pl.BlockSpec(memory_space=pl.ANY)
    wide, narrow = (span_count, planes, cols), (span_count, planes, slots)
    nodes = [domains >> level for level in range(4)]
    levels = [(node, planes, slots) for node in nodes]
    fields = [(planes, cells)] + [(planes, cells + 2 * LANES)] * 2 + [(16, cells)] * 2
    shapes = [wide, narrow, narrow, wide, wide, narrow, narrow, narrow] + levels + levels + [levels[3]]
    return pl.pallas_call(
        functools.partial(spectral_kernel, span_count),
        out_shape=(jax.ShapeDtypeStruct(scalar.shape, scalar.dtype),) * 2,
        in_specs=[vmem] * 8 + [hbm] * 4,
        out_specs=(vmem, vmem),
        scratch_shapes=[pltpu.VMEM(shape, jnp.float32) for shape in fields]
        + [pltpu.VMEM(block.shape, block.dtype) for block in blocks]
        + [pltpu.VMEM(shape, jnp.float32) for shape in shapes]
        + [
            pltpu.SemaphoreType.DMA((4,)),
            pltpu.SemaphoreType.DMA((5, span_count - 1)),
            pltpu.SemaphoreType.DMA((5, span_count - 1)),
            pltpu.SemaphoreType.DMA((2,)),
            pltpu.SemaphoreType.DMA((2, 2, 3)),
        ],
        compiler_params=pltpu.CompilerParams(
            collective_id=0, has_side_effects=True, vmem_limit_bytes=40 * 2**20
        ),
    )(scalar, vel, weight, near, table, diagonal, shift, interface, *blocks)


def on_device(
    scalar,
    span_vel,
    flux_weight,
    neighbours,
    diagonal,
    interface,
    schur_one,
    schur_two,
    schur_three,
    schur_root,
):
    waves = jnp.arange(PLANES, dtype=jnp.int32)
    table = fourier_entry(waves[:, None], waves[None, :])
    shift = wave_shift(waves)[:, None]
    blocks = (schur_one, schur_two, schur_three, schur_root)
    return projected(
        scalar,
        span_vel,
        flux_weight,
        neighbours,
        table,
        diagonal[None, :],
        shift,
        interface,
        blocks,
        lax.axis_size("span"),
    )


def solution(mesh):
    placed = (
        P(("case", "span"), "dom"),
        P(("case", "span"), "dom"),
        P(None, "dom"),
        P(None, "dom"),
        P("dom"),
        P("dom", None),
        P("span", "dom", None, None),
        P("span", "dom", None, None),
        P("span", "dom", None, None),
        P("span", None, None, None),
    )
    return jax.shard_map(
        on_device,
        mesh=mesh,
        in_specs=placed,
        out_specs=(P(("case", "span"), "dom"), P(("case", "span"), "dom")),
        check_vma=False,
    )
```
